128 devices in a mesh: row: 16 (over x, y), col: 8 (over z, core).
Axes of the slice: x: 4, y: 4, z: 4, core: 2. Of those that a mesh axis runs over, the one named last changes fastest.
Arguments:
- voltage: bfloat16 [16, 8, 2048, 256], P('row', 'col'), may hold values from -6 to 6
- sources: bfloat16 [16, 8, 2048, 256], P('row', 'col'), may hold values from -6 to 6
- capacity: float32 [16, 8, 2048], P('row', 'col'), may hold values from 0.1 to 1
- inverse: bfloat16 [16, 8, 2048, 2048], P('row', 'col')
- couple: bfloat16 [16, 8, 256, 2048], P('row', 'col'), may hold values from -0.125 to 0.125
- boundary: int32 [16, 8, 256], P('row', 'col'), may hold values from 0 to 2047, as said below
- panels: bfloat16 [16, 8, 7, 16, 3, 128, 128], P('row', 'col'), may hold values from -0.125 to 0.125
- pattern: int32 [16, 8, 7, 16, 3], P('row', 'col'), may hold values from 0 to 15
Outputs:
- settled: float32 [16, 8, 2048, 256], P('row', 'col')
The draws below stay inside these ranges and needn't reach their ends.
Inputs may be any that keep to these rules, and one draw needn't show every extreme that they name: `boundary`: the 256 indices of one subdomain are distinct.
All inputs are finite; a program needn't handle non-finite values.
Results may differ from the reference program's by a relative error of at most 0.007.
Values may be sent and summed in bfloat16 or wider, within the bound.
No kernel may reach another device: no remote copies, remote signals or barrier semaphores. Data moves between devices by JAX's collectives and lax.ppermute only.
A program may use at most 128 MiB of HBM per device.

```python
import math
import jax
import jax.numpy as jnp
from jax import lax

NI = 2048
BLK = 128
KB = 3
NBND = 256
RHS = 256
STEPS = 2
NB = 16
LEVELS = 7
N_ROW = 16
N_COL = 8


def draw_inverse(key, part):
    key_off = jax.random.fold_in(key, 11)
    key_diag = jax.random.fold_in(key, 12)
    shape = (N_ROW, N_COL, NI, NI)
    off = jax.random.normal(key_off, shape, jnp.float32) * (0.4 / NI ** 0.5)
    diag = jax.random.uniform(key_diag, (N_ROW, N_COL, NI), jnp.float32, 0.3, 0.6)
    eye = jnp.eye(NI, dtype=jnp.float32)
    full = off + diag[..., None] * eye
    return full.astype(jnp.bfloat16)


def draw_boundary(key, part):
    keys = jax.random.split(jax.random.fold_in(key, 21), N_ROW * N_COL)
    picked = jax.vmap(lambda one: jax.random.permutation(one, NI)[:NBND])(keys)
    return picked.reshape(N_ROW, N_COL, NBND).astype(jnp.int32)


def place_ends(entries, rng, least, top_value):
    extent = entries.shape
    place = [jax.random.randint(jax.random.fold_in(rng, axis), (), 0, extent[axis]) for axis in range(len(extent))]
    entries = entries.at[tuple(place)].set(least)
    longest = extent.index(max(extent))
    place[longest] = (place[longest] + 1) % extent[longest]
    return entries.at[tuple(place)].set(top_value)


def block_scale(key, dims, pieces, smallest, top_value):
    def one(position, parts):
        draws = jax.random.uniform(jax.random.fold_in(jax.random.fold_in(key, 6), position), (parts,), jnp.float32, smallest / len(pieces), top_value / len(pieces))
        return jnp.repeat(jnp.exp(draws), dims[position] // parts).reshape((-1,) + (1,) * (len(dims) - position - 1))

    level = one(*pieces[0])
    for cut in pieces[1:]:
        level = level * one(*cut)
    return level


def noise(key, extent, deviation, bound, cuts=(), held_as=jnp.bfloat16):
    factor_of = block_scale(key, extent, cuts, -0.22, 0.18) if cuts else 1.0
    drawn = jax.random.normal(key, extent, jnp.float32) * deviation * factor_of
    return jnp.minimum(jnp.maximum(drawn, -bound), bound).astype(held_as)


def setup_inputs(seed: int = 0) -> dict:
    splits = jax.random.split(jax.random.key(seed), 9)
    voltage = noise(splits[0], (N_ROW, N_COL, NI, RHS), 1.0, 6.0, ((0, 16), (1, 8)))
    sources = noise(splits[1], (N_ROW, N_COL, NI, RHS), 1.0, 6.0, ((0, 16), (1, 8)))
    capacity = jnp.clip(jnp.exp(math.log(1.0) - 2.3025851 * jax.random.uniform(splits[2], (N_ROW, N_COL, NI), jnp.float32) ** block_scale(splits[2], (N_ROW, N_COL, NI), ((0, 16), (1, 8)), -0.2, 0.2)), 0.1, 1.0)
    inverse = draw_inverse(jax.random.fold_in(splits[8], 71), 0)
    couple = noise(splits[4], (N_ROW, N_COL, NBND, N_COL * NBND), (N_COL * NBND) ** -0.5, 0.125, ((0, 16), (1, 8)))
    boundary = draw_boundary(jax.random.fold_in(splits[8], 71), 0)
    panels = noise(splits[6], (N_ROW, N_COL, LEVELS, NB, KB, BLK, BLK), (KB * BLK * 6) ** -0.5, 0.125, ((0, 16), (1, 8)))
    pattern = place_ends(jax.random.randint(splits[7], (N_ROW, N_COL, LEVELS, NB, KB), 0, NB), jax.random.fold_in(splits[7], 1), 0, NB - 1).astype(jnp.int32)
    return {"voltage": voltage, "sources": sources, "capacity": capacity, "inverse": inverse, "couple": couple, "boundary": boundary, "panels": panels, "pattern": pattern}


def merge_level(merged, panels_level, pattern_level, level):
    devices = N_ROW * N_COL
    stride = 2 ** level
    sent = merged.astype(jnp.bfloat16)
    partner = sent.reshape(devices // (2 * stride), 2, stride, NI, RHS)[:, ::-1].reshape(devices, NI, RHS)

    def apply_panel(items):
        received, blocks, columns = items
        tiles = received.reshape(NB, BLK, RHS)
        picked = tiles[columns].astype(jnp.float32)
        update = jnp.einsum("nkij,nkjr->nir", blocks.astype(jnp.float32), picked)
        return update.reshape(NI, RHS)

    update = lax.map(apply_panel, (partner, panels_level, pattern_level))
    return merged + update


def reference(voltage, sources, capacity, inverse, couple, boundary, panels, pattern):
    devices = N_ROW * N_COL
    potential = voltage.astype(jnp.float32).reshape(devices, NI, RHS)
    source_flat = sources.astype(jnp.float32).reshape(devices, NI, RHS)
    cap_flat = capacity.reshape(devices, NI, 1)
    index_flat = boundary.reshape(devices, NBND).astype(jnp.int32)
    inverse_flat = inverse.reshape(devices, NI, NI)
    panel_flat = panels.reshape(devices, LEVELS, NB, KB, BLK, BLK)
    pattern_flat = pattern.reshape(devices, LEVELS, NB, KB).astype(jnp.int32)
    weights = couple.astype(jnp.float32)
    device_ids = jnp.arange(devices, dtype=jnp.int32)[:, None]
    for step in range(STEPS):
        edge = potential[device_ids, index_flat].astype(jnp.bfloat16)
        edge_rows = edge.reshape(N_ROW, N_COL * NBND, RHS).astype(jnp.float32)
        coupled = jnp.einsum("rcbk,rkn->rcbn", weights, edge_rows).reshape(devices, NBND, RHS)
        base = cap_flat * potential + source_flat
        loaded = base.at[device_ids, index_flat].add(coupled).astype(jnp.bfloat16)
        merged = lax.map(lambda items: jnp.dot(items[0], items[1], preferred_element_type=jnp.float32), (inverse_flat, loaded))
        for level in range(LEVELS):
            merged = merge_level(merged, panel_flat[:, level], pattern_flat[:, level], level)
        potential = merged
    return potential.reshape(N_ROW, N_COL, NI, RHS)
```

```python
import jax
import jax.numpy as jnp
from jax import lax
from jax.experimental import pallas as pl
from jax.experimental.pallas import tpu as pltpu
from jax.sharding import PartitionSpec as P

NI = 2048
BLK = 128
NB = 16
NBND = 256
RHS = 256
STEPS = 2
LEVELS = 7
N_COL = 8
SIZES = (64, 64, 64, 64)

NN = (((1,), (0,)), ((), ()))
NT = (((1,), (1,)), ((), ()))
F32 = jnp.float32
BF16 = jnp.bfloat16


def mm(a, b, dims):
    return lax.dot_general(a, b, dims, preferred_element_type=F32)


def lanes(ref, first, count):
    return jnp.concatenate([ref[first + j] for j in range(count)], axis=1)


def prepare_kernel(volt_ref, src_ref, cap_ref, bnd_ref, *outs):
    count = len(SIZES)
    hot_ref = outs[0]
    bases, sources, edges = outs[1 : 1 + count], outs[1 + count : 1 + 2 * count], outs[1 + 2 * count :]
    eye = (
        lax.broadcasted_iota(jnp.int32, (RHS, RHS), 0) == lax.broadcasted_iota(jnp.int32, (RHS, RHS), 1)
    ).astype(F32).astype(BF16)
    index = bnd_ref[...]
    edge = jnp.zeros((RHS, NBND), F32)
    for j in range(NB):
        rows = pl.ds(j * BLK, BLK)
        hot = (lax.broadcasted_iota(jnp.int32, (NBND, BLK), 1) + j * BLK == index).astype(F32).astype(BF16)
        hot_ref[:, rows] = hot
        volt = mm(eye, volt_ref[rows, :], NT)
        src = mm(eye, src_ref[rows, :], NT)
        edge = edge + mm(volt.astype(BF16), hot, NT)
        base = cap_ref[:, rows] * volt + src
        start = 0
        for q, size in enumerate(SIZES):
            bases[q][j] = base[start : start + size]
            sources[q][j] = src[start : start + size].astype(BF16)
            start += size
    start = 0
    for q, size in enumerate(SIZES):
        edges[q][...] = edge[start : start + size].astype(BF16)
        start += size


def interior_kernel(edge_ref, couple_ref, hot_ref, base_ref, inv_ref, m_ref, send_ref):
    size = base_ref.shape[1]
    edge = jnp.concatenate([edge_ref[d] for d in range(N_COL)], axis=1)
    coupled = mm(edge, couple_ref[...], NT)
    high = coupled.astype(BF16)
    low = (coupled - high.astype(F32)).astype(BF16)
    hot = hot_ref[...]
    base = lanes(base_ref, 0, NB)
    loaded = (base + (mm(high, hot, NN) + mm(low, hot, NN))).astype(BF16)
    for n in range(NB // 2):
        part = mm(loaded, inv_ref[pl.ds(2 * BLK * n, 2 * BLK), :], NT)
        for h in range(2):
            piece = part[:, h * BLK : (h + 1) * BLK]
            m_ref[2 * n + h] = piece
            send_ref[2 * n + h] = piece.astype(BF16)


def merged_block(level, i, pat_ref, m_ref, recv_ref, pan_ref):
    got = jnp.concatenate([recv_ref[pat_ref[level, i, k]] for k in range(3)], axis=1)
    blocks = jnp.concatenate([pan_ref[level, i, k] for k in range(3)], axis=1)
    return m_ref[i] + mm(got, blocks, NT)


def level_kernel(level, pat_ref, m_ref, recv_ref, pan_ref, out_ref, send_ref):
    for i in range(NB):
        new = merged_block(level, i, pat_ref, m_ref, recv_ref, pan_ref)
        out_ref[i] = new
        send_ref[i] = new.astype(BF16)


def turn_kernel(level, pat_ref, m_ref, recv_ref, pan_ref, src_ref, cap_ref, hot_ref, base_ref, edge_ref):
    size = m_ref.shape[1]
    rounded = []
    for i in range(NB):
        rows = pl.ds(i * BLK, BLK)
        new = merged_block(level, i, pat_ref, m_ref, recv_ref, pan_ref)
        rounded.append(new.astype(BF16))
        base_ref[i] = cap_ref[:, rows] * new + src_ref[i].astype(F32)
    edge_ref[...] = mm(jnp.concatenate(rounded, axis=1), hot_ref[...], NT).astype(BF16)


def last_kernel(level, pat_ref, m_ref, recv_ref, pan_ref, out_ref):
    for i in range(NB):
        out_ref[i] = merged_block(level, i, pat_ref, m_ref, recv_ref, pan_ref)


def finish_kernel(*refs):
    parts, out_ref = refs[:-1], refs[-1]
    for i in range(NB):
        whole = jnp.concatenate([part[i] for part in parts], axis=0)
        out_ref[pl.ds(i * BLK, BLK), :] = whole.T


VM = pl.BlockSpec(memory_space=pltpu.VMEM)
SM = pl.BlockSpec(memory_space=pltpu.SMEM)


def call(kernel, name, ins, outs, flops, nbytes):
    specs = [SM if x.dtype == jnp.int32 and x.ndim == 3 else VM for x in ins]
    ins = [x if x.dtype == jnp.int32 else pltpu.with_memory_space_constraint(x, pltpu.VMEM) for x in ins]
    return pl.pallas_call(
        kernel,
        name=name,
        out_shape=outs,
        in_specs=specs,
        out_specs=[VM] * len(outs),
        compiler_params=pltpu.CompilerParams(vmem_limit_bytes=24 * 1024 * 1024),
        cost_estimate=pl.CostEstimate(flops=flops, bytes_accessed=nbytes, transcendentals=0),
    )(*ins)


def vmem(shape, dtype):
    return pltpu.VMEM(shape, dtype)


def level_cost(size):
    return 2 * NB * 3 * BLK * BLK * 256, 1 << 20


def exchanged(x, level):
    mask = 1 << level
    pairs = [(d, d ^ mask) for d in range(128)]
    return lax.ppermute(x, ("row", "col"), pairs)


def per_device(voltage, sources, capacity, inverse, couple, boundary, panels, pattern):
    voltage, sources, inverse, couple = voltage[0, 0], sources[0, 0], inverse[0, 0], couple[0, 0]
    cap = capacity[0, 0].reshape(1, NI)
    index = boundary[0, 0].reshape(NBND, 1)
    panels, pattern = panels[0, 0], pattern[0, 0]
    count = len(SIZES)
    prepared = call(
        prepare_kernel,
        "prepare",
        [voltage, sources, cap, index],
        [vmem((NBND, NI), BF16)]
        + [vmem((NB, s, BLK), F32) for s in SIZES]
        + [vmem((NB, s, BLK), BF16) for s in SIZES]
        + [vmem((s, NBND), BF16) for s in SIZES],
        1 << 30,
        4 << 20,
    )
    hot = prepared[0]
    bases = prepared[1 : 1 + count]
    srcs = prepared[1 + count : 1 + 2 * count]
    edges = prepared[1 + 2 * count :]
    done = [None] * count
    for q, s in enumerate(SIZES):
        base, edge = bases[q], edges[q]
        for step in range(STEPS):
            gathered = lax.all_gather(edge, "col", axis=0)
            m, send = call(
                interior_kernel,
                f"interior{step}_{q}",
                [gathered, couple, hot, base, inverse],
                [vmem((NB, s, BLK), F32), vmem((NB, s, BLK), BF16)],
                2 * NI * NI * 256,
                4 << 20,
            )
            for level in range(LEVELS):
                recv = exchanged(send, level)
                name = f"level{step}_{level}_{q}"
                args = [pattern, m, recv, panels]
                if level < LEVELS - 1:
                    def kern(*r, level=level):
                        level_kernel(level, *r)
                    m, send = call(
                        kern, name, args, [vmem((NB, s, BLK), F32), vmem((NB, s, BLK), BF16)], *level_cost(s)
                    )
                elif step < STEPS - 1:
                    def kern(*r, level=level):
                        turn_kernel(level, *r)
                    base, edge = call(
                        kern,
                        name,
                        args + [srcs[q], cap, hot],
                        [vmem((NB, s, BLK), F32), vmem((s, NBND), BF16)],
                        *level_cost(s),
                    )
                else:
                    def kern(*r, level=level):
                        last_kernel(level, *r)
                    (done[q],) = call(kern, name, args, [vmem((NB, s, BLK), F32)], *level_cost(s))
    (out,) = pl.pallas_call(
        finish_kernel,
        name="finish",
        out_shape=[jax.ShapeDtypeStruct((NI, RHS), F32)],
        in_specs=[VM] * count,
        out_specs=[VM],
        compiler_params=pltpu.CompilerParams(vmem_limit_bytes=24 * 1024 * 1024),
    )(*[pltpu.with_memory_space_constraint(x, pltpu.VMEM) for x in done])
    return out[None, None]


def solution(mesh):
    return jax.shard_map(
        per_device,
        mesh=mesh,
        in_specs=(
            P("row", "col", None, None),
            P("row", "col", None, None),
            P("row", "col", None),
            P("row", "col", None, None),
            P("row", "col", None, None),
            P("row", "col", None),
            P("row", "col", None, None, None, None, None),
            P("row", "col", None, None, None),
        ),
        out_specs=P("row", "col", None, None),
        check_vma=False,
    )
```

```python
import jax
import jax.numpy as jnp
from jax import lax
from jax.experimental import pallas as pl
from jax.experimental.pallas import tpu as pltpu
from jax.sharding import PartitionSpec as P

NI = 2048
BLK = 128
KB = 3
NB = 16
NBND = 256
RHS = 256
STEPS = 2
LEVELS = 7
N_COL = 8
TABLE = LEVELS * NB * KB
SIZES = (64, 64, 64, 64)
STAGGER = 1.3

NN = (((1,), (0,)), ((), ()))
NT = (((1,), (1,)), ((), ()))
F32 = jnp.float32
BF16 = jnp.bfloat16
VM = pl.BlockSpec(memory_space=pltpu.VMEM)
SM = pl.BlockSpec(memory_space=pltpu.SMEM)


def mm(a, b, dims):
    return lax.dot_general(a, b, dims, preferred_element_type=F32)


def joined(ref, first, count):
    return jnp.concatenate([ref[first + j] for j in range(count)], axis=1)


def eye():
    rows = lax.broadcasted_iota(jnp.int32, (RHS, RHS), 0)
    return (rows == lax.broadcasted_iota(jnp.int32, (RHS, RHS), 1)).astype(F32).astype(BF16)


def first_kernel(volt_ref, bnd_ref, pat_ref, col_ref, hot_ref, flip_ref, edge_ref, table_ref):
    one = eye()
    index = bnd_ref[...]
    edge = jnp.zeros((RHS, NBND), F32)
    for j in range(NB // 2):
        rows = pl.ds(2 * j * BLK, 2 * BLK)
        nodes = lax.broadcasted_iota(jnp.int32, (2 * BLK, NBND), 0) + 2 * j * BLK
        hot = (nodes == index).astype(F32).astype(BF16)
        hot_ref[rows, :] = hot
        flipped = mm(one, volt_ref[rows, :], NT).astype(BF16)
        edge = edge + mm(flipped, hot, NN)
        flip_ref[2 * j] = flipped[:, :BLK]
        flip_ref[2 * j + 1] = flipped[:, BLK:]
    edge_ref[...] = edge.astype(BF16)
    for k in range(TABLE):
        table_ref[k] = pat_ref[k]
    table_ref[TABLE] = col_ref[0]


def start_kernel(src_ref, cap_ref, flip_ref, inv_ref, m_ref, *flipped_refs):
    one = eye()
    parts = []
    for j in range(NB):
        rows = pl.ds(j * BLK, BLK)
        src = mm(one, src_ref[rows, :], NT)
        parts.append((cap_ref[:, rows] * flip_ref[j].astype(F32) + src).astype(BF16))
        first = 0
        for ref in flipped_refs:
            size = ref.shape[1]
            ref[j] = src[first : first + size].astype(BF16)
            first += size
    loaded = jnp.concatenate(parts, axis=1)
    product(loaded, inv_ref, m_ref)


def product(loaded, inv_ref, m_ref):
    for n in range(NB // 2):
        part = mm(loaded, inv_ref[pl.ds(2 * BLK * n, 2 * BLK), :], NT)
        m_ref[2 * n] = part[:, :BLK]
        m_ref[2 * n + 1] = part[:, BLK:]


def response_kernel(inv_ref, hot_ref, out_ref):
    for n in range(NB // 2):
        rows = pl.ds(2 * BLK * n, 2 * BLK)
        out_ref[rows, :] = mm(inv_ref[rows, :], hot_ref[...], NN).astype(BF16)


def interior_kernel(base_ref, inv_ref, m_ref):
    product(joined(base_ref, 0, NB), inv_ref, m_ref)


def coupled_of(table_ref, edge_refs, couple_ref):
    col = table_ref[TABLE]
    coupled = jnp.zeros((edge_refs[0].shape[0], NBND), F32)
    for mask, ref in enumerate(edge_refs):
        owner = pl.multiple_of(lax.bitwise_xor(col, mask) * NBND, NBND)
        coupled = coupled + mm(ref[...], couple_ref[:, pl.ds(owner, NBND)], NT)
    return coupled.astype(BF16)


def correct_all_kernel(table_ref, couple_ref, resp_ref, m_ref, *refs):
    edge_refs, outs = refs[:N_COL], refs[N_COL:]
    count = len(outs) // 2
    coupled = coupled_of(table_ref, edge_refs, couple_ref)
    for i in range(NB):
        new = m_ref[i] + mm(coupled, resp_ref[pl.ds(i * BLK, BLK), :], NT)
        first = 0
        for q in range(count):
            size = outs[q].shape[1]
            piece = new[first : first + size]
            outs[q][i] = piece
            outs[count + q][i] = piece.astype(BF16)
            first += size


def correct_kernel(table_ref, couple_ref, resp_ref, m_ref, *refs):
    edge_refs, (out_ref, send_ref) = refs[:N_COL], refs[N_COL:]
    coupled = coupled_of(table_ref, edge_refs, couple_ref)
    for i in range(NB):
        new = m_ref[i] + mm(coupled, resp_ref[pl.ds(i * BLK, BLK), :], NT)
        out_ref[i] = new
        send_ref[i] = new.astype(BF16)


def merged_block(level, i, table_ref, m_ref, recv_ref, pan_ref):
    at = (level * NB + i) * KB
    got = jnp.concatenate([recv_ref[table_ref[at + k]] for k in range(KB)], axis=1)
    blocks = jnp.concatenate([pan_ref[level, i, k] for k in range(KB)], axis=1)
    return m_ref[i] + mm(got, blocks, NT)


def level_kernel(level, table_ref, m_ref, recv_ref, pan_ref, out_ref, send_ref):
    for i in range(NB):
        new = merged_block(level, i, table_ref, m_ref, recv_ref, pan_ref)
        out_ref[i] = new
        send_ref[i] = new.astype(BF16)


def turn_kernel(level, table_ref, m_ref, recv_ref, pan_ref, src_ref, cap_ref, hot_ref, base_ref, edge_ref):
    rounded = []
    for i in range(NB):
        new = merged_block(level, i, table_ref, m_ref, recv_ref, pan_ref)
        rounded.append(new.astype(BF16))
        base_ref[i] = (cap_ref[:, pl.ds(i * BLK, BLK)] * new + src_ref[i].astype(F32)).astype(BF16)
    edge_ref[...] = mm(jnp.concatenate(rounded, axis=1), hot_ref[...], NN).astype(BF16)


def last_kernel(level, table_ref, m_ref, recv_ref, pan_ref, out_ref):
    for i in range(NB):
        out_ref[i] = merged_block(level, i, table_ref, m_ref, recv_ref, pan_ref)


def finish_kernel(*refs):
    parts, out_ref = refs[:-1], refs[-1]
    for i in range(NB):
        whole = jnp.concatenate([part[i] for part in parts], axis=0)
        out_ref[pl.ds(i * BLK, BLK), :] = whole.T


class Order:
    def __init__(self):
        self.token = None

    def __call__(self, kernel, name, ins, outs, flops=1 << 27):
        specs, args = [], []
        for x in ins:
            scalar = x.dtype == jnp.int32 and x.ndim == 1
            specs.append(SM if scalar else VM)
            args.append(x if scalar else pltpu.with_memory_space_constraint(x, pltpu.VMEM))
        count = len(args)
        chained = self.token is not None
        if chained:
            specs.append(VM)
            args.append(pltpu.with_memory_space_constraint(self.token, pltpu.VMEM))

        def body(*refs):
            kernel(*refs[:count], *refs[count + chained : -1])
            refs[-1][...] = jnp.zeros((8, 128), F32)

        results = pl.pallas_call(
            body,
            name=name,
            out_shape=[*outs, pltpu.VMEM((8, 128), F32)],
            in_specs=specs,
            out_specs=[SM if getattr(o, "memory_space", None) == pltpu.SMEM else VM for o in outs] + [VM],
            compiler_params=pltpu.CompilerParams(vmem_limit_bytes=20 * 1024 * 1024),
            cost_estimate=pl.CostEstimate(flops=flops, bytes_accessed=1 << 20, transcendentals=0),
        )(*args)
        self.token = results[-1]
        return results[:-1]


def moved(x, mask):
    return lax.ppermute(x, ("row", "col"), [(d, d ^ mask) for d in range(128)])


def edges_of(edge):
    got = [edge] + [None] * (N_COL - 1)
    for mask in (2, 4, 6):
        got[mask] = moved(edge, mask)
    for mask in (0, 2, 4, 6):
        got[mask + 1] = moved(got[mask], 1)
    return got


def at_level(kernel, level):
    return lambda *refs: kernel(level, *refs)


def per_device(voltage, sources, capacity, inverse, couple, boundary, panels, pattern):
    voltage, sources, inverse, couple = voltage[0, 0], sources[0, 0], inverse[0, 0], couple[0, 0]
    cap = capacity[0, 0].reshape(1, NI)
    index = boundary[0, 0].reshape(1, NBND)
    panels = panels[0, 0]
    pattern = pattern[0, 0].reshape(TABLE)
    column = lax.axis_index("col").reshape(1)
    count = len(SIZES)
    V = pltpu.VMEM
    run = Order()

    hot, flip, edge, table = run(
        first_kernel,
        "first",
        [voltage, index, pattern, column],
        [V((NI, NBND), BF16), V((NB, RHS, BLK), BF16), V((RHS, NBND), BF16), pltpu.SMEM((TABLE + 8,), jnp.int32)],
    )
    edges = edges_of(edge)
    m, *srcs = run(
        start_kernel,
        "start",
        [sources, cap, flip, inverse],
        [V((NB, RHS, BLK), F32)] + [V((NB, s, BLK), BF16) for s in SIZES],
        flops=3 << 30,
    )
    (resp,) = run(response_kernel, "response", [inverse, hot], [V((NI, NBND), BF16)], flops=2 << 30)
    outs = run(
        correct_all_kernel,
        "correct_all",
        [table, couple, resp, m, *edges],
        [V((NB, s, BLK), F32) for s in SIZES] + [V((NB, s, BLK), BF16) for s in SIZES],
        flops=1 << 29,
    )

    def chain(q):
        s = SIZES[q]
        m, send = outs[q], outs[count + q]
        state = [V((NB, s, BLK), F32), V((NB, s, BLK), BF16)]
        for step in range(STEPS):
            for level in range(LEVELS):
                recv = moved(send, 1 << level)
                yield max(level, 0.3) + 7 * step
                name = f"level{step}_{level}_{q}"
                args = [table, m, recv, panels]
                if level < LEVELS - 1:
                    m, send = run(at_level(level_kernel, level), name, args, state)
                elif step < STEPS - 1:
                    base, edge = run(
                        at_level(turn_kernel, level),
                        name,
                        args + [srcs[q], cap, hot],
                        [V((NB, s, BLK), BF16), V((s, NBND), BF16)],
                    )
                    edges = edges_of(edge)
                    yield level + 0.4 + 7 * step
                    (m,) = run(interior_kernel, f"interior{step}_{q}", [base, inverse], state[:1], flops=2 << 30)
                    yield level + 1 + 7 * step
                    m, send = run(correct_kernel, f"correct{step}_{q}", [table, couple, resp, m, *edges], state)
                else:
                    (done[q],) = run(at_level(last_kernel, level), name, args, state[:1])

    done = [None] * count
    chains = [chain(q) for q in range(count)]
    places = [next(c) + STAGGER * q for q, c in enumerate(chains)]
    while any(p is not None for p in places):
        q = min((p, q) for q, p in enumerate(places) if p is not None)[1]
        place = next(chains[q], None)
        places[q] = None if place is None else place + STAGGER * q
    (out,) = pl.pallas_call(
        finish_kernel,
        name="finish",
        out_shape=[jax.ShapeDtypeStruct((NI, RHS), F32)],
        in_specs=[VM] * count,
        out_specs=[VM],
        compiler_params=pltpu.CompilerParams(vmem_limit_bytes=20 * 1024 * 1024),
    )(*[pltpu.with_memory_space_constraint(x, pltpu.VMEM) for x in done])
    return out[None, None]


def solution(mesh):
    return jax.shard_map(
        per_device,
        mesh=mesh,
        in_specs=(
            P("row", "col", None, None),
            P("row", "col", None, None),
            P("row", "col", None),
            P("row", "col", None, None),
            P("row", "col", None, None),
            P("row", "col", None),
            P("row", "col", None, None, None, None, None),
            P("row", "col", None, None, None),
        ),
        out_specs=P("row", "col", None, None),
        check_vma=False,
    )
```

```python
import jax
import jax.numpy as jnp
from jax import lax
from jax.experimental import pallas as pl
from jax.experimental.pallas import tpu as pltpu
from jax.sharding import PartitionSpec as P

NI = 2048
BLK = 128
KB = 3
NB = 16
NBND = 256
RHS = 256
STEPS = 2
LEVELS = 7
N_COL = 8
TABLE = LEVELS * NB * KB
SIZES = (64, 64, 64, 64)
STAGGER = 1.3
ORDER = (1, 3, 0, 1, 0, 1, 2, 0, 3, 1, 2, 0, 1, 3, 0, 2, 1, 3, 0, 2, 1, 3, 1, 0, 2, 1, 3, 0, 0, 2, 1, 0, 3, 1, 3, 0, 1, 2, 2, 3, 2, 0, 2, 3, 1, 0, 2, 3, 1, 2, 0, 3, 1, 2, 0, 3, 1, 2, 0, 3, 1, 2, 0, 3, 2, 0, 3, 1, 2, 3, 2, 3)

MIB = 1 << 20
RATE = 1000000000
NN = (((1,), (0,)), ((), ()))
NT = (((1,), (1,)), ((), ()))
F32 = jnp.float32
BF16 = jnp.bfloat16
VM = pl.BlockSpec(memory_space=pltpu.VMEM)
SM = pl.BlockSpec(memory_space=pltpu.SMEM)


def mm(a, b, dims):
    return lax.dot_general(a, b, dims, preferred_element_type=F32)


def joined(ref, first, count):
    return jnp.concatenate([ref[first + j] for j in range(count)], axis=1)


def eye():
    rows = lax.broadcasted_iota(jnp.int32, (RHS, RHS), 0)
    return (rows == lax.broadcasted_iota(jnp.int32, (RHS, RHS), 1)).astype(F32).astype(BF16)


def first_kernel(volt_ref, bnd_ref, hot_ref, flip_ref, edge_ref):
    one = eye()
    index = bnd_ref[...]
    edge = jnp.zeros((RHS, NBND), F32)
    for j in range(NB // 2):
        rows = pl.ds(2 * j * BLK, 2 * BLK)
        nodes = lax.broadcasted_iota(jnp.int32, (2 * BLK, NBND), 0) + 2 * j * BLK
        hot = (nodes == index).astype(F32).astype(BF16)
        hot_ref[rows, :] = hot
        flipped = mm(one, volt_ref[rows, :], NT).astype(BF16)
        edge = edge + mm(flipped, hot, NN)
        flip_ref[2 * j] = flipped[:, :BLK]
        flip_ref[2 * j + 1] = flipped[:, BLK:]
    edge_ref[...] = edge.astype(BF16)


def start_kernel(src_ref, cap_ref, flip_ref, inv_ref, hot_ref, pat_ref, now_ref, m_ref, resp_ref, table_ref, *flipped):
    one = eye()
    parts = []
    for j in range(NB // 2):
        rows = pl.ds(2 * j * BLK, 2 * BLK)
        src = mm(one, src_ref[rows, :], NT)
        parts.append((cap_ref[:, rows] * joined(flip_ref, 2 * j, 2).astype(F32) + src).astype(BF16))
        first = 0
        for ref in flipped:
            size = ref.shape[1]
            for h in range(2):
                ref[2 * j + h] = src[first : first + size, h * BLK : (h + 1) * BLK].astype(BF16)
            first += size
    product(jnp.concatenate(parts, axis=1), inv_ref, m_ref)
    for n in range(NB // 2):
        rows = pl.ds(2 * BLK * n, 2 * BLK)
        resp_ref[rows, :] = mm(inv_ref[rows, :], hot_ref[...], NN).astype(BF16)
    for k in range(TABLE):
        table_ref[k] = pat_ref[k]
    table_ref[TABLE] = now_ref[0]


def product(loaded, inv_ref, m_ref):
    for n in range(NB // 2):
        part = mm(loaded, inv_ref[pl.ds(2 * BLK * n, 2 * BLK), :], NT)
        m_ref[2 * n] = part[:, :BLK]
        m_ref[2 * n + 1] = part[:, BLK:]


def interior_kernel(base_ref, inv_ref, m_ref):
    product(joined(base_ref, 0, NB), inv_ref, m_ref)


def pair_kernel(edge_ref, recv_ref, out_ref):
    out_ref[0] = edge_ref[...]
    out_ref[1] = recv_ref[...]


def four_kernel(pair_ref, recv_ref, out_ref):
    out_ref[:2] = pair_ref[...]
    out_ref[2:] = recv_ref[...]


def coupled_of(table_ref, edges, couple_ref):
    coupled = jnp.zeros((edges[0].shape[0], NBND), F32)
    for mask, edge in enumerate(edges):
        owner = pl.multiple_of(lax.bitwise_xor(table_ref[TABLE], mask) * NBND, NBND)
        coupled = coupled + mm(edge, couple_ref[:, pl.ds(owner, NBND)], NT)
    return coupled.astype(BF16)


def row_kernel(*refs):
    for k, ref in enumerate(refs[:-1]):
        refs[-1][k] = ref[...]


def correct_all_kernel(table_ref, couple_ref, resp_ref, m_ref, own_ref, other_ref, *outs):
    count = len(outs) // 2
    edges = [ref[k] for k in range(N_COL // 2) for ref in (own_ref, other_ref)]
    coupled = coupled_of(table_ref, edges, couple_ref)
    for i in range(NB // 2):
        new = mm(coupled, resp_ref[pl.ds(2 * i * BLK, 2 * BLK), :], NT)
        for h in range(2):
            half = m_ref[2 * i + h] + new[:, h * BLK : (h + 1) * BLK]
            first = 0
            for q in range(count):
                size = outs[q].shape[1]
                piece = half[first : first + size]
                outs[q][2 * i + h] = piece
                outs[count + q][2 * i + h] = piece.astype(BF16)
                first += size


def correct_kernel(table_ref, couple_ref, resp_ref, m_ref, own_ref, other_ref, out_ref, send_ref):
    edges = [ref[k] for k in range(N_COL // 2) for ref in (own_ref, other_ref)]
    coupled = coupled_of(table_ref, edges, couple_ref)
    for i in range(NB // 2):
        new = mm(coupled, resp_ref[pl.ds(2 * i * BLK, 2 * BLK), :], NT)
        for h in range(2):
            half = m_ref[2 * i + h] + new[:, h * BLK : (h + 1) * BLK]
            out_ref[2 * i + h] = half
            send_ref[2 * i + h] = half.astype(BF16)


def merged_block(level, i, table_ref, m_ref, recv_ref, pan_ref):
    got = jnp.concatenate([recv_ref[table_ref[(level * NB + i) * KB + k]] for k in range(KB)], axis=1)
    blocks = jnp.concatenate([pan_ref[level, i, k] for k in range(KB)], axis=1)
    return m_ref[i] + mm(got, blocks, NT)


def level_kernel(level, table_ref, m_ref, recv_ref, pan_ref, out_ref, send_ref):
    for i in range(NB):
        new = merged_block(level, i, table_ref, m_ref, recv_ref, pan_ref)
        out_ref[i] = new
        send_ref[i] = new.astype(BF16)


def turn_kernel(level, table_ref, m_ref, recv_ref, pan_ref, src_ref, cap_ref, hot_ref, base_ref, edge_ref):
    rounded = []
    for i in range(NB):
        new = merged_block(level, i, table_ref, m_ref, recv_ref, pan_ref)
        rounded.append(new.astype(BF16))
        base_ref[i] = (cap_ref[:, pl.ds(i * BLK, BLK)] * new + src_ref[i].astype(F32)).astype(BF16)
    edge_ref[...] = mm(jnp.concatenate(rounded, axis=1), hot_ref[...], NN).astype(BF16)


def last_kernel(level, table_ref, m_ref, recv_ref, pan_ref, out_ref):
    for i in range(NB):
        out_ref[i] = merged_block(level, i, table_ref, m_ref, recv_ref, pan_ref)


def finish_kernel(*refs):
    parts, out_ref = refs[:-1], refs[-1]
    for i in range(NB):
        whole = jnp.concatenate([part[i] for part in parts], axis=0)
        out_ref[pl.ds(i * BLK, BLK), :] = whole.T


class Order:
    def __init__(self):
        self.token = None

    def __call__(self, kernel, name, ins, outs, limit=4, cost=0.8):
        specs, args = [], []
        for x in ins:
            scalar = x.dtype == jnp.int32 and x.ndim == 1
            specs.append(SM if scalar else VM)
            args.append(x if scalar else pltpu.with_memory_space_constraint(x, pltpu.VMEM))
        count = len(args)
        chained = self.token is not None
        if chained:
            specs.append(VM)
            args.append(pltpu.with_memory_space_constraint(self.token, pltpu.VMEM))

        last = count + chained + len(outs)

        def body(*refs):
            kernel(*refs[:count], *refs[count + chained : last])
            refs[last][...] = jnp.zeros((8, 128), F32)

        results = pl.pallas_call(
            body,
            name=name,
            out_shape=[*outs, pltpu.VMEM((8, 128), F32)],
            in_specs=specs,
            out_specs=[SM if getattr(o, "memory_space", None) == pltpu.SMEM else VM for o in outs] + [VM],
            compiler_params=pltpu.CompilerParams(vmem_limit_bytes=limit * MIB),
            cost_estimate=pl.CostEstimate(flops=int(cost * RATE), bytes_accessed=1024, transcendentals=0),
        )(*args)
        self.token = results[-1]
        return results[:-1]


def moved(x, mask):
    return lax.ppermute(x, ("row", "col"), [(d, d ^ mask) for d in range(128)])


def at_level(kernel, level):
    return lambda *refs: kernel(level, *refs)


def per_device(voltage, sources, capacity, inverse, couple, boundary, panels, pattern):
    voltage, sources, inverse, couple = voltage[0, 0], sources[0, 0], inverse[0, 0], couple[0, 0]
    cap = capacity[0, 0].reshape(1, NI)
    index = boundary[0, 0].reshape(1, NBND)
    panels = panels[0, 0]
    pattern = pattern[0, 0].reshape(TABLE)
    column = lax.axis_index("col").reshape(1)
    count = len(SIZES)
    V = pltpu.VMEM
    run = Order()

    hot, flip, edge = run(
        first_kernel,
        "first",
        [voltage, index],
        [V((NI, NBND), BF16), V((NB, RHS, BLK), BF16), V((RHS, NBND), BF16)],
    )
    edges = [edge] + [moved(edge, mask) for mask in (2, 4, 6)]
    m, resp, table, *srcs = run(
        start_kernel,
        "start",
        [sources, cap, flip, inverse, hot, pattern, column],
        [V((NB, RHS, BLK), F32), V((NI, NBND), BF16), pltpu.SMEM((TABLE + 8,), jnp.int32)]
        + [V((NB, s, BLK), BF16) for s in SIZES],
        limit=8,
        cost=8,
    )
    (own,) = run(row_kernel, "row", edges, [V((N_COL // 2, RHS, NBND), BF16)], cost=0.2)
    outs = run(
        correct_all_kernel,
        "correct_all",
        [table, couple, resp, m, own, moved(own, 1)],
        [V((NB, s, BLK), F32) for s in SIZES] + [V((NB, s, BLK), BF16) for s in SIZES],
    )

    def chain(q):
        s = SIZES[q]
        m, send = outs[q], outs[count + q]
        state = [V((NB, s, BLK), F32), V((NB, s, BLK), BF16)]
        for step in range(STEPS):
            for level in range(LEVELS):
                recv = moved(send, 1 << level)
                yield max(level, 0.3) + 7 * step
                name = f"level{step}_{level}_{q}"
                args = [table, m, recv, panels]
                if level < LEVELS - 1:
                    m, send = run(at_level(level_kernel, level), name, args, state)
                elif step < STEPS - 1:
                    base, edge = run(
                        at_level(turn_kernel, level),
                        name,
                        args + [srcs[q], cap, hot],
                        [V((NB, s, BLK), BF16), V((s, NBND), BF16)],
                    )
                    recv = moved(edge, 2)
                    yield level + 0.2 + 7 * step
                    (m,) = run(interior_kernel, f"interior{step}_{q}", [base, inverse], state[:1], cost=2.7)
                    yield level + 0.5 + 7 * step
                    (pair,) = run(pair_kernel, f"pair{step}_{q}", [edge, recv], [V((2, s, NBND), BF16)], cost=0.1)
                    recv = moved(pair, 4)
                    yield level + 0.8 + 7 * step
                    (own,) = run(four_kernel, f"four{step}_{q}", [pair, recv], [V((4, s, NBND), BF16)], cost=0.1)
                    other = moved(own, 1)
                    yield level + 1 + 7 * step
                    m, send = run(correct_kernel, f"correct{step}_{q}", [table, couple, resp, m, own, other], state, cost=1.3)
                else:
                    (done[q],) = run(at_level(last_kernel, level), name, args, state[:1])

    done = [None] * count
    chains = [chain(q) for q in range(count)]
    places = [next(c) + STAGGER * q for q, c in enumerate(chains)]
    for q in ORDER or ():
        places[q] = next(chains[q], None)
    while any(p is not None for p in places):
        q = min((p, q) for q, p in enumerate(places) if p is not None)[1]
        place = next(chains[q], None)
        places[q] = None if place is None else place + STAGGER * q
    (out,) = pl.pallas_call(
        finish_kernel,
        name="finish",
        out_shape=[jax.ShapeDtypeStruct((NI, RHS), F32)],
        in_specs=[VM] * count,
        out_specs=[VM],
        compiler_params=pltpu.CompilerParams(vmem_limit_bytes=8 * MIB),
    )(*[pltpu.with_memory_space_constraint(x, pltpu.VMEM) for x in done])
    return out[None, None]


def solution(mesh):
    return jax.shard_map(
        per_device,
        mesh=mesh,
        in_specs=(
            P("row", "col", None, None),
            P("row", "col", None, None),
            P("row", "col", None),
            P("row", "col", None, None),
            P("row", "col", None, None),
            P("row", "col", None),
            P("row", "col", None, None, None, None, None),
            P("row", "col", None, None, None),
        ),
        out_specs=P("row", "col", None, None),
        check_vma=False,
    )
```

```python
import jax
import jax.numpy as jnp
from jax import lax
from jax.experimental import pallas as pl
from jax.experimental.pallas import tpu as pltpu
from jax.sharding import PartitionSpec as P

NI = 2048
BLK = 128
KB = 3
NB = 16
NBND = 256
RHS = 256
STEPS = 2
LEVELS = 7
N_COL = 8
TABLE = LEVELS * NB * KB
SIZES = (64, 64, 64, 64)
STAGGER = 1.3
ORDER = (1, 3, 0, 1, 0, 1, 2, 0, 3, 1, 2, 0, 1, 3, 0, 2, 1, 3, 0, 2, 1, 3, 1, 0, 2, 1, 3, 0, 0, 2, 1, 0, 3, 1, 3, 0, 2, 1, 2, 3, 2, 0, 2, 1, 3, 3, 0, 2, 1, 2, 0, 3, 1, 2, 0, 3, 1, 2, 0, 3, 1, 2, 0, 3, 2, 0, 3, 1, 2, 3, 2, 3)

MIB = 1 << 20
RATE = 1000000000
NN = (((1,), (0,)), ((), ()))
NT = (((1,), (1,)), ((), ()))
F32 = jnp.float32
BF16 = jnp.bfloat16
VM = pl.BlockSpec(memory_space=pltpu.VMEM)
SM = pl.BlockSpec(memory_space=pltpu.SMEM)


def mm(a, b, dims):
    return lax.dot_general(a, b, dims, preferred_element_type=F32)


def joined(ref, first, count):
    return jnp.concatenate([ref[first + j] for j in range(count)], axis=1)


def eye():
    rows = lax.broadcasted_iota(jnp.int32, (RHS, RHS), 0)
    return (rows == lax.broadcasted_iota(jnp.int32, (RHS, RHS), 1)).astype(F32).astype(BF16)


def first_kernel(volt_ref, bnd_ref, hot_ref, flip_ref, edge_ref):
    one = eye()
    index = bnd_ref[...]
    edge = jnp.zeros((RHS, NBND), F32)
    for j in range(NB // 2):
        rows = pl.ds(2 * j * BLK, 2 * BLK)
        nodes = lax.broadcasted_iota(jnp.int32, (2 * BLK, NBND), 0) + 2 * j * BLK
        hot = (nodes == index).astype(F32).astype(BF16)
        hot_ref[rows, :] = hot
        flipped = mm(one, volt_ref[rows, :], NT).astype(BF16)
        edge = edge + mm(flipped, hot, NN)
        flip_ref[2 * j] = flipped[:, :BLK]
        flip_ref[2 * j + 1] = flipped[:, BLK:]
    edge_ref[...] = edge.astype(BF16)


def start_kernel(src_ref, cap_ref, flip_ref, inv_ref, hot_ref, pat_ref, now_ref, m_ref, resp_ref, table_ref, *flipped):
    one = eye()
    parts = []
    for j in range(NB // 2):
        rows = pl.ds(2 * j * BLK, 2 * BLK)
        src = mm(one, src_ref[rows, :], NT)
        parts.append((cap_ref[:, rows] * joined(flip_ref, 2 * j, 2).astype(F32) + src).astype(BF16))
        first = 0
        for ref in flipped:
            size = ref.shape[1]
            for h in range(2):
                ref[2 * j + h] = src[first : first + size, h * BLK : (h + 1) * BLK].astype(BF16)
            first += size
    product(jnp.concatenate(parts, axis=1), inv_ref, m_ref)
    for n in range(NB // 2):
        rows = pl.ds(2 * BLK * n, 2 * BLK)
        resp_ref[rows, :] = mm(inv_ref[rows, :], hot_ref[...], NN).astype(BF16)
    for k in range(TABLE):
        table_ref[k] = pat_ref[k]
    table_ref[TABLE] = now_ref[0]


def product(loaded, inv_ref, m_ref):
    for n in range(NB // 2):
        part = mm(loaded, inv_ref[pl.ds(2 * BLK * n, 2 * BLK), :], NT)
        m_ref[2 * n] = part[:, :BLK]
        m_ref[2 * n + 1] = part[:, BLK:]


def interior_kernel(base_ref, inv_ref, m_ref):
    product(joined(base_ref, 0, NB), inv_ref, m_ref)


def pair_kernel(edge_ref, recv_ref, out_ref):
    out_ref[0] = edge_ref[...]
    out_ref[1] = recv_ref[...]


def four_kernel(pair_ref, recv_ref, out_ref):
    out_ref[:2] = pair_ref[...]
    out_ref[2:] = recv_ref[...]


def coupled_of(table_ref, edges, couple_ref):
    coupled = jnp.zeros((edges[0].shape[0], NBND), F32)
    for mask, edge in enumerate(edges):
        owner = pl.multiple_of(lax.bitwise_xor(table_ref[TABLE], mask) * NBND, NBND)
        coupled = coupled + mm(edge, couple_ref[:, pl.ds(owner, NBND)], NT)
    return coupled.astype(BF16)


def row_kernel(*refs):
    for k, ref in enumerate(refs[:-1]):
        refs[-1][k] = ref[...]


def correct_all_kernel(table_ref, couple_ref, resp_ref, m_ref, own_ref, other_ref, *outs):
    count = len(outs) // 2
    edges = [ref[k] for k in range(N_COL // 2) for ref in (own_ref, other_ref)]
    coupled = coupled_of(table_ref, edges, couple_ref)
    for i in range(NB // 2):
        new = mm(coupled, resp_ref[pl.ds(2 * i * BLK, 2 * BLK), :], NT)
        for h in range(2):
            half = m_ref[2 * i + h] + new[:, h * BLK : (h + 1) * BLK]
            first = 0
            for q in range(count):
                size = outs[q].shape[1]
                piece = half[first : first + size]
                outs[q][2 * i + h] = piece
                outs[count + q][2 * i + h] = piece.astype(BF16)
                first += size


def correct_kernel(table_ref, couple_ref, resp_ref, m_ref, own_ref, other_ref, out_ref, send_ref):
    edges = [ref[k] for k in range(N_COL // 2) for ref in (own_ref, other_ref)]
    coupled = coupled_of(table_ref, edges, couple_ref)
    for i in range(NB // 2):
        new = mm(coupled, resp_ref[pl.ds(2 * i * BLK, 2 * BLK), :], NT)
        for h in range(2):
            half = m_ref[2 * i + h] + new[:, h * BLK : (h + 1) * BLK]
            out_ref[2 * i + h] = half
            send_ref[2 * i + h] = half.astype(BF16)


def merged_block(level, i, table_ref, m_ref, recv_ref, pan_ref):
    got = jnp.concatenate([recv_ref[table_ref[(level * NB + i) * KB + k]] for k in range(KB)], axis=1)
    blocks = jnp.concatenate([pan_ref[level, i, k] for k in range(KB)], axis=1)
    return m_ref[i] + mm(got, blocks, NT)


def level_kernel(level, table_ref, m_ref, recv_ref, pan_ref, out_ref, send_ref):
    for i in range(NB):
        new = merged_block(level, i, table_ref, m_ref, recv_ref, pan_ref)
        out_ref[i] = new
        send_ref[i] = new.astype(BF16)


def turn_kernel(level, table_ref, m_ref, recv_ref, pan_ref, src_ref, cap_ref, hot_ref, base_ref, edge_ref):
    rounded = []
    for i in range(NB):
        new = merged_block(level, i, table_ref, m_ref, recv_ref, pan_ref)
        rounded.append(new.astype(BF16))
        base_ref[i] = (cap_ref[:, pl.ds(i * BLK, BLK)] * new + src_ref[i].astype(F32)).astype(BF16)
    edge_ref[...] = mm(jnp.concatenate(rounded, axis=1), hot_ref[...], NN).astype(BF16)


def last_kernel(level, table_ref, m_ref, recv_ref, pan_ref, out_ref):
    for i in range(NB):
        out_ref[i] = merged_block(level, i, table_ref, m_ref, recv_ref, pan_ref)


def finish_kernel(*refs):
    parts, out_ref = refs[:-1], refs[-1]
    for i in range(NB):
        whole = jnp.concatenate([part[i] for part in parts], axis=0)
        out_ref[pl.ds(i * BLK, BLK), :] = whole.T


class Order:
    def __init__(self):
        self.token = None

    def __call__(self, kernel, name, ins, outs, limit=4, cost=0.8):
        specs, args = [], []
        for x in ins:
            scalar = x.dtype == jnp.int32 and x.ndim == 1
            specs.append(SM if scalar else VM)
            args.append(x if scalar else pltpu.with_memory_space_constraint(x, pltpu.VMEM))
        count = len(args)
        chained = self.token is not None
        if chained:
            specs.append(VM)
            args.append(pltpu.with_memory_space_constraint(self.token, pltpu.VMEM))

        last = count + chained + len(outs)

        def body(*refs):
            kernel(*refs[:count], *refs[count + chained : last])
            refs[last][...] = jnp.zeros((8, 128), F32)

        results = pl.pallas_call(
            body,
            name=name,
            out_shape=[*outs, pltpu.VMEM((8, 128), F32)],
            in_specs=specs,
            out_specs=[SM if getattr(o, "memory_space", None) == pltpu.SMEM else VM for o in outs] + [VM],
            compiler_params=pltpu.CompilerParams(vmem_limit_bytes=limit * MIB),
            cost_estimate=pl.CostEstimate(flops=int(cost * RATE), bytes_accessed=1024, transcendentals=0),
        )(*args)
        self.token = results[-1]
        return results[:-1]


def moved(x, mask):
    return lax.ppermute(x, ("row", "col"), [(d, d ^ mask) for d in range(128)])


def at_level(kernel, level):
    return lambda *refs: kernel(level, *refs)


def per_device(voltage, sources, capacity, inverse, couple, boundary, panels, pattern):
    voltage, sources, inverse, couple = voltage[0, 0], sources[0, 0], inverse[0, 0], couple[0, 0]
    cap = capacity[0, 0].reshape(1, NI)
    index = boundary[0, 0].reshape(1, NBND)
    panels = panels[0, 0]
    pattern = pattern[0, 0].reshape(TABLE)
    column = lax.axis_index("col").reshape(1)
    count = len(SIZES)
    V = pltpu.VMEM
    run = Order()

    hot, flip, edge = run(
        first_kernel,
        "first",
        [voltage, index],
        [V((NI, NBND), BF16), V((NB, RHS, BLK), BF16), V((RHS, NBND), BF16)],
    )
    edges = [edge] + [moved(edge, mask) for mask in (2, 4, 6)]
    m, resp, table, *srcs = run(
        start_kernel,
        "start",
        [sources, cap, flip, inverse, hot, pattern, column],
        [V((NB, RHS, BLK), F32), V((NI, NBND), BF16), pltpu.SMEM((TABLE + 8,), jnp.int32)]
        + [V((NB, s, BLK), BF16) for s in SIZES],
        limit=8,
        cost=8,
    )
    (own,) = run(row_kernel, "row", edges, [V((N_COL // 2, RHS, NBND), BF16)], cost=0.2)
    outs = run(
        correct_all_kernel,
        "correct_all",
        [table, couple, resp, m, own, moved(own, 1)],
        [V((NB, s, BLK), F32) for s in SIZES] + [V((NB, s, BLK), BF16) for s in SIZES],
    )

    def chain(q):
        s = SIZES[q]
        m, send = outs[q], outs[count + q]
        state = [V((NB, s, BLK), F32), V((NB, s, BLK), BF16)]
        for step in range(STEPS):
            for level in range(LEVELS):
                recv = moved(send, 1 << level)
                yield max(level, 0.3) + 7 * step
                name = f"level{step}_{level}_{q}"
                args = [table, m, recv, panels]
                if level < LEVELS - 1:
                    m, send = run(at_level(level_kernel, level), name, args, state)
                elif step < STEPS - 1:
                    base, edge = run(
                        at_level(turn_kernel, level),
                        name,
                        args + [srcs[q], cap, hot],
                        [V((NB, s, BLK), BF16), V((s, NBND), BF16)],
                    )
                    recv = moved(edge, 2)
                    yield level + 0.2 + 7 * step
                    (m,) = run(interior_kernel, f"interior{step}_{q}", [base, inverse], state[:1], cost=2.7)
                    yield level + 0.5 + 7 * step
                    (pair,) = run(pair_kernel, f"pair{step}_{q}", [edge, recv], [V((2, s, NBND), BF16)], cost=0.1)
                    recv = moved(pair, 4)
                    yield level + 0.8 + 7 * step
                    (own,) = run(four_kernel, f"four{step}_{q}", [pair, recv], [V((4, s, NBND), BF16)], cost=0.1)
                    other = moved(own, 1)
                    yield level + 1 + 7 * step
                    m, send = run(correct_kernel, f"correct{step}_{q}", [table, couple, resp, m, own, other], state, cost=1.3)
                else:
                    (done[q],) = run(at_level(last_kernel, level), name, args, state[:1])

    done = [None] * count
    chains = [chain(q) for q in range(count)]
    places = [next(c) + STAGGER * q for q, c in enumerate(chains)]
    for q in ORDER or ():
        places[q] = next(chains[q], None)
    while any(p is not None for p in places):
        q = min((p, q) for q, p in enumerate(places) if p is not None)[1]
        place = next(chains[q], None)
        places[q] = None if place is None else place + STAGGER * q
    (out,) = pl.pallas_call(
        finish_kernel,
        name="finish",
        out_shape=[jax.ShapeDtypeStruct((NI, RHS), F32)],
        in_specs=[VM] * count,
        out_specs=[VM],
        compiler_params=pltpu.CompilerParams(vmem_limit_bytes=8 * MIB),
    )(*[pltpu.with_memory_space_constraint(x, pltpu.VMEM) for x in done])
    return out[None, None]


def solution(mesh):
    return jax.shard_map(
        per_device,
        mesh=mesh,
        in_specs=(
            P("row", "col", None, None),
            P("row", "col", None, None),
            P("row", "col", None),
            P("row", "col", None, None),
            P("row", "col", None, None),
            P("row", "col", None),
            P("row", "col", None, None, None, None, None),
            P("row", "col", None, None, None),
        ),
        out_specs=P("row", "col", None, None),
        check_vma=False,
    )
```
